32 devices in a mesh: pole: 2 (over y), prow: 4 (over z), pcol: 4 (over x, core).
Axes of the slice: x: 2, y: 2, z: 4, core: 2. Of those that a mesh axis runs over, the one named last changes fastest.
Arguments:
- inverse_block: bfloat16 [2, 4096, 2048], P(None, ('pole', 'prow'), 'pcol'), parts along dimension 1, may hold values from -6 to 6
- factor_column: bfloat16 [4096, 2, 1024], P(('pole', 'prow')), parts along dimension 0, may hold values from -0.125 to 0.125
- block_pattern: int32 [4, 16], P('pole', 'prow'), parts along dimension 0, may hold values 0 or 1
- pivot_inverse: float32 [4, 2, 512, 512], P('pole'), parts along dimension 0, may hold values from -6 to 6
Outputs:
- selected_column: float32 [4096, 2, 1024], P(('pole', 'prow', 'pcol')), parts along dimension 0
- selected_pivot: float32 [4, 2, 512, 512], P('pole'), parts along dimension 0
The draws below stay inside these ranges and needn't reach their ends.
There are 2 independent parts, one for each index of `pole`. The reference program is written for one: setup_inputs(seed, part) draws one part's arguments, and reference() takes and returns one part's arrays. A program takes and returns all parts, laid end to end along the dimension named above; each array names one. Nothing has to cross between parts.
All inputs are finite; a program needn't handle non-finite values. No bound on the sum of `block_pattern` on one device may be relied on, other than what follows from the above.
Results may differ from the reference program's by a relative error of at most 0.0025.
Values may be sent and summed in bfloat16 or wider, within the bound.
No kernel may reach another device: no remote copies, remote signals or barrier semaphores. Data moves between devices by JAX's collectives and lax.ppermute only.
A program may use at most 64 MiB of HBM per device.

```python
import jax
import jax.numpy as jnp
from jax import lax

S = 512
BLK = 128
NC = 2048


def place_ends(array, key, smallest, top_value):
    longest = array.shape.index(max(array.shape))
    spots = []
    for shift in (0, 1):
        where = [jax.random.randint(jax.random.fold_in(key, axis), (), 0, length) for axis, length in enumerate(array.shape)]
        where[longest] = (where[longest] + shift) % array.shape[longest]
        spots.append(tuple(where))
    return array.at[spots[0]].set(smallest).at[spots[1]].set(top_value)


def steps_of(own_key, extent, cuts, smallest, largest):
    level = 1.0
    for dim, blocks in cuts:
        draws = jax.random.uniform(jax.random.fold_in(jax.random.fold_in(own_key, 6), dim), (blocks,), jnp.float32, smallest / len(cuts), largest / len(cuts))
        level = level * jnp.repeat(jnp.exp(draws), extent[dim] // blocks).reshape((-1,) + (1,) * (len(extent) - 1 - dim))
    return level


def scatter_about(key, shape, deviation, bound, shards=(), held_as=jnp.bfloat16):
    gain = steps_of(key, shape, shards, -0.22, 0.18) if shards else 1.0
    drawn = jax.random.normal(key, shape, jnp.float32) * deviation * gain
    return jnp.minimum(jnp.maximum(drawn, -bound), bound).astype(held_as)


def setup_inputs(seed: int = 0, part: int = 0) -> dict:
    key_of = jax.random.split(jax.random.key(seed), 5)
    part_keys = jax.random.split(jax.random.fold_in(key_of[4], part), 5)
    return {
        "inverse_block": scatter_about(part_keys[0], (2, NC, NC), 1.0, 6.0, ((1, 4), (2, 4))),
        "factor_column": scatter_about(part_keys[1], (NC, 2, 2 * S), NC ** -0.5, 0.125, ((0, 4),)),
        "block_pattern": place_ends((jax.random.randint(part_keys[2], (2, NC // BLK), 0, 4) < 3).astype(jnp.int32), jax.random.fold_in(part_keys[2], 1), 0, 1),
        "pivot_inverse": scatter_about(part_keys[3], (2, 2, S, S), 1.0, 6.0, (), jnp.float32),
    }


def expand_pattern(block_pattern):
    blocks = block_pattern.shape[1]
    keep_rows = block_pattern.T.astype(jnp.bfloat16)
    keep_rows = jnp.broadcast_to(keep_rows[:, None, :, None], (blocks, BLK, 2, S))
    return keep_rows.reshape(blocks * BLK, 1, 2 * S)


def complex_column(inverse_real, inverse_imag, factor):
    row_total = inverse_real.shape[0]
    flat = factor.reshape(factor.shape[0], 4 * S)
    real_part = jnp.dot(inverse_real, flat, preferred_element_type=jnp.float32).reshape(row_total, 2, 2 * S)
    imag_part = jnp.dot(inverse_imag, flat, preferred_element_type=jnp.float32).reshape(row_total, 2, 2 * S)
    real_out = real_part[:, 0] - imag_part[:, 1]
    imag_out = real_part[:, 1] + imag_part[:, 0]
    return -jnp.stack([real_out, imag_out], axis=1)


def reference(inverse_block, factor_column, block_pattern, pivot_inverse):
    masked = factor_column * expand_pattern(block_pattern)
    selected_column = complex_column(inverse_block[0], inverse_block[1], masked)
    chosen = selected_column.astype(jnp.bfloat16).astype(jnp.float32).reshape(NC, 2, 2, S)
    parts = masked.astype(jnp.float32).reshape(NC, 2, 2, S)
    m_real = parts[:, 0]
    m_imag = parts[:, 1]
    left = jnp.stack([jnp.stack([m_real, m_imag], axis=1), jnp.stack([-m_imag, m_real], axis=1)], axis=1)
    outer = jnp.einsum("rqojs,rqjt->jost", left, chosen, precision=lax.Precision.HIGHEST)
    selected_pivot = pivot_inverse - outer
    return selected_column, selected_pivot
```

```python
import jax
import jax.numpy as jnp
from jax import lax
from jax.sharding import PartitionSpec as P

S = 512
BLK = 128


def swap(x, axis, distance):
    size = lax.axis_size(axis)
    return lax.ppermute(x, axis, [(i, i ^ distance) for i in range(size)])


def gather_z(m):
    size = lax.axis_size("prow")
    if size != 4:
        return [(m, 0)] + [(swap(m, "prow", d), d) for d in range(1, size)]
    level = lax.axis_index("prow")
    two = swap(m, "prow", 2)
    one = swap(m, "prow", 1)
    middle = lax.ppermute(m, "prow", [(1, 2), (2, 1)])
    ends = lax.ppermute(two, "prow", [(2, 3), (1, 0)])
    inner = (level == 1) | (level == 2)
    return [(m, 0), (one, 1), (two, 2), (jnp.where(inner, middle, ends), 3)]


def gather_col(a):
    size = lax.axis_size("pcol")
    across = [(a, 0)] + [(swap(a, "pcol", d), d) for d in range(2, size, 2)]
    return across + [(swap(piece, "pcol", 1), d ^ 1) for piece, d in across]


def per_device(inverse_block, factor_column, block_pattern, pivot_inverse):
    bf16 = jnp.bfloat16
    levels = lax.axis_size("prow")
    level = lax.axis_index("prow")
    columns = lax.axis_size("pcol")
    column = lax.axis_index("pcol")
    rows = factor_column.shape[0]
    width = factor_column.shape[2] // columns
    blocks = rows // BLK
    node = column * width // S

    keep = lax.dynamic_index_in_dim(block_pattern, node, 0, keepdims=False).astype(bf16)
    keep = jnp.broadcast_to(keep[:, None], (blocks, BLK)).reshape(1, rows, 1)
    own = lax.dynamic_slice_in_dim(factor_column, column * width, width, 2)
    own = jnp.transpose(own, (1, 0, 2)) * keep
    side = lax.dynamic_slice_in_dim(factor_column, node * S, S, 2)
    side = jnp.transpose(side, (1, 0, 2)) * keep

    a_pieces = gather_col(inverse_block)
    m_pieces = gather_z(own)
    depth = inverse_block.shape[2]
    a_all = jnp.zeros((2, rows, depth * columns), bf16)
    for piece, d in a_pieces:
        a_all = lax.dynamic_update_slice(a_all, piece, (0, 0, (column ^ d) * depth))
    m_all = jnp.zeros((2, rows * levels, width), bf16)
    for piece, d in m_pieces:
        m_all = lax.dynamic_update_slice(m_all, piece, (0, (level ^ d) * rows, 0))
    dot = lambda a, b: jnp.dot(a, b, preferred_element_type=jnp.float32)
    right = jnp.concatenate([m_all[0], m_all[1]], axis=1)
    turned = jnp.concatenate([-m_all[1], m_all[0]], axis=1)
    y = -(dot(a_all[0], right) + dot(a_all[1], turned))
    chosen = y.astype(bf16)
    yr, yi = chosen[:, :width], chosen[:, width:]
    dot_t = lambda a, b: lax.dot_general(a, b, (((0,), (0,)), ((), ())), preferred_element_type=jnp.float32)
    part = dot_t(side[0], chosen) + dot_t(side[1], jnp.concatenate([-yi, yr], axis=1))
    share = S // levels
    part = part.reshape(levels, share, 2 * width)

    def take(i):
        return lax.dynamic_index_in_dim(part, i, 0, keepdims=False)

    total = take(level)
    for d in range(1, levels):
        total = total + swap(take(level ^ d).astype(bf16), "prow", d).astype(jnp.float32)
    piece = total.astype(bf16)

    cut = rows // columns
    y_parts = y.reshape(columns, cut, 2 * width)
    y_all = lax.all_to_all(y_parts, "pcol", 0, 0)
    own_rows = jnp.transpose(y_all.reshape(columns, cut, 2, width), (1, 2, 0, 3)).reshape(cut, 2, columns * width)

    nodes = pivot_inverse.shape[0]
    minus = jnp.zeros((columns, levels, share, 2 * width), bf16)
    for p, d in [(piece, 0)] + [(swap(piece, "prow", d), d) for d in range(1, levels)]:
        for q, e in gather_col(p):
            minus = lax.dynamic_update_slice(minus, q[None, None], (column ^ e, level ^ d, 0, 0))
    minus = minus.reshape(nodes, columns // nodes, S, 2, width)
    minus = jnp.transpose(minus, (0, 3, 2, 1, 4)).reshape(nodes, 2, S, S)
    return own_rows, pivot_inverse - minus.astype(jnp.float32)


def solution(mesh):
    in_specs = (
        P(None, ("pole", "prow"), "pcol"),
        P(("pole", "prow"), None, None),
        P("pole", "prow"),
        P("pole", None, None, None),
    )
    out_specs = (P(("pole", "prow", "pcol"), None, None), P("pole", None, None, None))
    return jax.shard_map(
        per_device, mesh=mesh, in_specs=in_specs, out_specs=out_specs, check_vma=False
    )
```

```python
import functools

import jax
import jax.numpy as jnp
from jax import lax
from jax.experimental import pallas as pl
from jax.experimental.pallas import tpu as pltpu
from jax.sharding import PartitionSpec as P

S = 512
BLK = 128
VMEM_LIMIT = 48 * 1024 * 1024
bf16 = jnp.bfloat16
f32 = jnp.float32


def swap(x, axis, distance):
    size = lax.axis_size(axis)
    return lax.ppermute(x, axis, [(i, i ^ distance) for i in range(size)])


def gather_z(m):
    size = lax.axis_size("prow")
    if size != 4:
        return [m] + [swap(m, "prow", d) for d in range(1, size)]
    level = lax.axis_index("prow")
    two = swap(m, "prow", 2)
    one = swap(m, "prow", 1)
    middle = lax.ppermute(m, "prow", [(1, 2), (2, 1)])
    ends = lax.ppermute(two, "prow", [(2, 3), (1, 0)])
    inner = (level == 1) | (level == 2)
    return [m, one, two, jnp.where(inner, middle, ends)]


def gather_col(a):
    size = lax.axis_size("pcol")
    across = {0: a}
    for e in range(2, size, 2):
        across[e] = swap(a, "pcol", e)
    for e in range(0, size, 2):
        across[e ^ 1] = swap(across[e], "pcol", 1)
    return [across[e] for e in range(size)]


def dot(a, b):
    return jnp.dot(a, b, preferred_element_type=f32)


def turn(m):
    width = m.shape[1] // 2
    return jnp.concatenate([-m[:, width:], m[:, :width]], axis=1)


def call(body, out_shape, scalars, operands, specs, out_specs, scratch=(), flops=0, aliases=None):
    return pl.pallas_call(
        body,
        out_shape=out_shape,
        grid_spec=pltpu.PrefetchScalarGridSpec(
            num_scalar_prefetch=1,
            grid=(1,),
            in_specs=specs,
            out_specs=out_specs,
            scratch_shapes=scratch,
        ),
        input_output_aliases=aliases or {},
        compiler_params=pltpu.CompilerParams(vmem_limit_bytes=VMEM_LIMIT),
        cost_estimate=pl.CostEstimate(flops=flops, bytes_accessed=4 << 20, transcendentals=0),
    )(scalars, *operands)


def whole(x):
    return pl.BlockSpec(x.shape, lambda i, ids, n=len(x.shape): (0,) * n)


def add_products(a_all, pieces, distances, ids):
    rows, wide = pieces[0].shape
    count = len(pieces)

    def body(ids_ref, *refs):
        total = None
        for a_ref, m_ref in zip(refs[:count], refs[count : 2 * count]):
            m = m_ref[...]
            term = dot(a_ref[0], m) + dot(a_ref[1], turn(m))
            total = term if total is None else total + term
        refs[-1][...] = total

    a_specs = [
        pl.BlockSpec((2, rows, rows), lambda i, ids, d=d: (0, 0, ids[0] ^ d)) for d in distances
    ]
    shape = jax.ShapeDtypeStruct((rows, wide), f32)
    return call(
        body,
        shape,
        ids,
        [a_all] * count + list(pieces),
        a_specs + [whole(m) for m in pieces],
        whole(shape),
        flops=4 * count * rows * rows * wide,
    )


def finish_products(a_all, piece, distance, total, side, ids, levels, columns):
    rows, wide = piece.shape
    cut = rows // columns
    share = S // levels

    def body(ids_ref, a_ref, m_ref, total_ref, side_ref, *refs):
        y_out = refs[:columns]
        p_out = refs[columns : columns + levels]
        y_ref, p_ref = refs[columns + levels :]
        m = m_ref[...]
        y_ref[...] = -(total_ref[...] + dot(a_ref[0], m) + dot(a_ref[1], turn(m)))
        chosen = y_ref[...].astype(bf16)
        p_ref[...] = dot(side_ref[0], chosen) + dot(side_ref[1], turn(chosen))
        for d in range(levels):
            start = pl.multiple_of((ids_ref[0] ^ d) * share, share)
            p_out[d][...] = p_ref[pl.ds(start, share), :].astype(p_out[d].dtype)
        for e in range(columns):
            start = pl.multiple_of((ids_ref[1] ^ e) * cut, cut)
            y_out[e][...] = y_ref[pl.ds(start, cut), :]

    shapes = [jax.ShapeDtypeStruct((cut, wide), f32)] * columns
    shapes += [jax.ShapeDtypeStruct((share, wide), f32 if d == 0 else bf16) for d in range(levels)]
    out = call(
        body,
        shapes,
        ids,
        [a_all, piece, total, side],
        [
            pl.BlockSpec((2, rows, rows), lambda i, ids: (0, 0, ids[0] ^ distance)),
            whole(piece),
            whole(total),
            whole(side),
        ],
        [whole(s) for s in shapes],
        [pltpu.VMEM((rows, wide), f32), pltpu.VMEM((S, wide), f32)],
        flops=4 * rows * wide * (rows + S),
    )
    return out[:columns], out[columns:]


def lay_rows(pieces, ids):
    cut, wide = pieces[0].shape
    width = wide // 2
    columns = len(pieces)

    def body(ids_ref, *refs):
        for e in range(columns):
            start = pl.multiple_of((ids_ref[1] ^ e) * width, width)
            for part in range(2):
                refs[-1][:, part, pl.ds(start, width)] = refs[e][:, part * width : (part + 1) * width]

    shape = jax.ShapeDtypeStruct((cut, 2, columns * width), f32)
    return call(body, shape, ids, pieces, [whole(p) for p in pieces], whole(shape))


def take_off(pivot, groups, flip, ids, rest=None):
    flat = [p for group in groups for p in group]
    share, wide = flat[0].shape
    width = wide // 2
    per_node = S // width
    levels = len(groups[0])

    def body(ids_ref, pivot_ref, *refs):
        out_ref = refs[-1]
        for n, ref in enumerate(refs[: len(flat)]):
            e, d = n // levels, n % levels
            top = pl.multiple_of((ids_ref[0] ^ d) * share, share)
            left = pl.multiple_of(((ids_ref[1] ^ e) % per_node) * width, width)
            for part in range(2):
                at = (0, part, pl.ds(top, share), pl.ds(left, width))
                out_ref[at] = pivot_ref[at] - ref[:, part * width : (part + 1) * width].astype(f32)

    spec = pl.BlockSpec((1, 2, S, S), lambda i, ids: (ids[2] ^ flip, 0, 0, 0))
    operands, specs, aliases = [pivot] + flat, [spec] + [whole(p) for p in flat], {}
    if rest is not None:
        operands, specs = operands + [rest], specs + [pl.BlockSpec(memory_space=pl.ANY)]
        aliases = {len(operands): 0}
    return call(
        body, jax.ShapeDtypeStruct(pivot.shape, f32), ids, operands, specs, spec, aliases=aliases
    )


def per_device(inverse_block, factor_column, block_pattern, pivot_inverse):
    levels = lax.axis_size("prow")
    level = lax.axis_index("prow")
    columns = lax.axis_size("pcol")
    column = lax.axis_index("pcol")
    rows = factor_column.shape[0]
    width = factor_column.shape[2] // columns
    per_node = S // width
    blocks = rows // BLK
    node = column // per_node
    ids = jnp.stack([level, column, node]).astype(jnp.int32)

    keep = lax.dynamic_index_in_dim(block_pattern, node, 0, keepdims=False).astype(bf16)
    keep = jnp.broadcast_to(keep[:, None], (blocks, BLK)).reshape(rows, 1, 1)
    own = lax.dynamic_slice_in_dim(factor_column, column * width, width, 2) * keep
    own = own.reshape(rows, 2 * width)
    m_pieces = gather_z(own)
    own, inverse_block = lax.optimization_barrier((own, inverse_block))
    a_pieces = gather_col(inverse_block)
    side = lax.dynamic_slice_in_dim(factor_column, node * S, S, 2) * keep
    side = jnp.transpose(side, (1, 2, 0))

    depth = inverse_block.shape[2]
    a_all = jnp.zeros((2, rows, depth * columns), bf16)
    for e, piece in enumerate(a_pieces):
        a_all = lax.dynamic_update_slice(a_all, piece, (0, 0, (column ^ e) * depth))
    total = add_products(a_all, m_pieces[:-1], range(levels - 1), ids)
    y_parts, p_parts = finish_products(
        a_all, m_pieces[-1], levels - 1, total, side, ids, levels, columns
    )

    sums = p_parts[0]
    for d in range(1, levels):
        sums = sums + swap(p_parts[d], "prow", d).astype(f32)
    sums = sums.astype(bf16)
    own_rows = lay_rows(
        [y_parts[0]] + [swap(y_parts[e], "pcol", e) for e in range(1, columns)], ids
    )

    pieces = [sums] + [swap(sums, "prow", d) for d in range(1, levels)]
    by_column = [gather_col(p) for p in pieces]
    groups = [[by_column[d][e] for d in range(levels)] for e in range(columns)]
    pivot = take_off(pivot_inverse, groups[:per_node], 0, ids)
    pivot = take_off(pivot_inverse, groups[per_node:], 1, ids, pivot)
    return own_rows, pivot


def solution(mesh):
    in_specs = (
        P(None, ("pole", "prow"), "pcol"),
        P(("pole", "prow"), None, None),
        P("pole", "prow"),
        P("pole", None, None, None),
    )
    out_specs = (P(("pole", "prow", "pcol"), None, None), P("pole", None, None, None))
    return jax.shard_map(
        per_device, mesh=mesh, in_specs=in_specs, out_specs=out_specs, check_vma=False
    )
```

```python
import functools

import jax
import jax.numpy as jnp
from jax import lax
from jax.experimental import pallas as pl
from jax.experimental.pallas import tpu as pltpu
from jax.sharding import PartitionSpec as P

S = 512
BLK = 128
COST = 1 << 16
VMEM_LIMIT = 48 * 1024 * 1024
bf16 = jnp.bfloat16
f32 = jnp.float32


def swap(x, axis, distance):
    size = lax.axis_size(axis)
    return lax.ppermute(x, axis, [(i, i ^ distance) for i in range(size)])


def gather_z(m, beside):
    size = lax.axis_size("prow")
    pieces = {0: m}
    step = size // 2
    while step > 1:
        pieces |= {d ^ step: swap(p, "prow", step) for d, p in pieces.items()}
        step //= 2
    far = pieces.copy()
    pieces |= {d ^ 1: swap(p, "prow", 1) for d, p in far.items() if d != size - 2}
    pieces, beside = lax.optimization_barrier((pieces, beside))
    last = swap(pieces[size - 2], "prow", 1)
    return [pieces[d] for d in range(size - 1)], last, beside


def gather_x(a):
    size = lax.axis_size("pcol")
    return {e: swap(a, "pcol", e) for e in range(2, size, 2)}


def gather_core(a):
    return [p for e in sorted(a) for p in (a[e], swap(a[e], "pcol", 1))]


def dot(a, b):
    return jnp.dot(a, b, preferred_element_type=f32)


def turn(m):
    width = m.shape[1] // 2
    return jnp.concatenate([-m[:, width:], m[:, :width]], axis=1)


def call(body, out_shape, scalars, operands, specs, out_specs, scratch=(), aliases=None):
    return pl.pallas_call(
        body,
        out_shape=out_shape,
        grid_spec=pltpu.PrefetchScalarGridSpec(
            num_scalar_prefetch=1,
            grid=(1,),
            in_specs=specs,
            out_specs=out_specs,
            scratch_shapes=scratch,
        ),
        input_output_aliases=aliases or {},
        compiler_params=pltpu.CompilerParams(vmem_limit_bytes=VMEM_LIMIT),
        cost_estimate=pl.CostEstimate(flops=0, bytes_accessed=COST, transcendentals=0),
    )(scalars, *operands)


def whole(x):
    return pl.BlockSpec(x.shape, lambda i, ids, n=len(x.shape): (0,) * n)


def add_products(a_pieces, m_pieces, ids, levels):
    rows, wide = m_pieces[0].shape
    columns = len(a_pieces)
    per = levels // columns

    def body(ids_ref, *refs):
        a_refs, m_refs = refs[:columns], refs[columns : columns + levels - 1]
        total_ref, left_ref, m_all = refs[columns + levels - 1 :]
        missing = ids_ref[0] ^ (levels - 1)
        for d, m_ref in enumerate(m_refs):
            m_all[ids_ref[0] ^ d] = m_ref[...]
        total_ref[...] = jnp.zeros_like(total_ref)
        for e, a_ref in enumerate(a_refs):
            for n in range(per):
                at = (ids_ref[1] ^ e) * per + n
                cut = slice(n * rows, (n + 1) * rows)

                @pl.when(at != missing)
                def _():
                    m = m_all[at]
                    total_ref[...] += dot(a_ref[0, :, cut], m) + dot(a_ref[1, :, cut], turn(m))

                @pl.when(at == missing)
                def _():
                    left_ref[...] = a_ref[:, :, cut]

    shapes = [jax.ShapeDtypeStruct((rows, wide), f32), jax.ShapeDtypeStruct((2, rows, rows), bf16)]
    return call(
        body,
        shapes,
        ids,
        list(a_pieces) + list(m_pieces),
        [whole(x) for x in a_pieces] + [whole(m) for m in m_pieces],
        [whole(x) for x in shapes],
        [pltpu.VMEM((levels, rows, wide), bf16)],
    )


def finish_products(left, last, total, side, ids, levels, columns):
    rows, wide = last.shape
    cut = rows // columns
    share = S // levels

    def body(ids_ref, a_ref, m_ref, total_ref, side_ref, *refs):
        y_out = refs[:columns]
        p_out = refs[columns : columns + levels]
        y_ref, p_ref = refs[columns + levels :]
        m = m_ref[...]
        y_ref[...] = -(total_ref[...] + dot(a_ref[0], m) + dot(a_ref[1], turn(m)))
        chosen = y_ref[...].astype(bf16)
        p_ref[...] = dot(side_ref[0], chosen) + dot(side_ref[1], turn(chosen))
        for d in range(levels):
            start = pl.multiple_of((ids_ref[0] ^ d) * share, share)
            p_out[d][...] = p_ref[pl.ds(start, share), :].astype(p_out[d].dtype)
        for e in range(columns):
            start = pl.multiple_of((ids_ref[1] ^ e) * cut, cut)
            y_out[e][...] = y_ref[pl.ds(start, cut), :]

    shapes = [jax.ShapeDtypeStruct((cut, wide), f32)] * columns
    shapes += [jax.ShapeDtypeStruct((share, wide), f32 if d == 0 else bf16) for d in range(levels)]
    out = call(
        body,
        shapes,
        ids,
        [left, last, total, side],
        [whole(x) for x in (left, last, total, side)],
        [whole(s) for s in shapes],
        [pltpu.VMEM((rows, wide), f32), pltpu.VMEM((S, wide), f32)],
    )
    return out[:columns], out[columns:]


def lay_rows(pieces, ids):
    cut, wide = pieces[0].shape
    width = wide // 2
    columns = len(pieces)

    def body(ids_ref, *refs):
        for e in range(columns):
            start = pl.multiple_of((ids_ref[1] ^ e) * width, width)
            for part in range(2):
                refs[-1][:, part, pl.ds(start, width)] = refs[e][:, part * width : (part + 1) * width]

    shape = jax.ShapeDtypeStruct((cut, 2, columns * width), f32)
    return call(body, shape, ids, pieces, [whole(p) for p in pieces], whole(shape))


def take_off(pivot, groups, flip, ids, rest=None):
    flat = [p for group in groups for p in group]
    wide = flat[0].shape[1]
    width = wide // 2
    per_node = S // width
    share = flat[0].shape[0]

    def body(ids_ref, pivot_ref, *refs):
        out_ref = refs[-1]
        n = 0
        for e, group in enumerate(groups):
            left = pl.multiple_of(((ids_ref[1] ^ e) % per_node) * width, width)
            d = 0
            for stack in group:
                for start in range(0, stack.shape[0], share):
                    top = pl.multiple_of((ids_ref[0] ^ d) * share, share)
                    for part in range(2):
                        at = (0, part, pl.ds(top, share), pl.ds(left, width))
                        piece = refs[n][start : start + share, part * width : (part + 1) * width]
                        out_ref[at] = pivot_ref[at] - piece.astype(f32)
                    d += 1
                n += 1

    spec = pl.BlockSpec((1, 2, S, S), lambda i, ids: (ids[2] ^ flip, 0, 0, 0))
    operands, specs, aliases = [pivot] + flat, [spec] + [whole(p) for p in flat], {}
    if rest is not None:
        operands, specs = operands + [rest], specs + [pl.BlockSpec(memory_space=pl.ANY)]
        aliases = {len(operands): 0}
    return call(
        body, jax.ShapeDtypeStruct(pivot.shape, f32), ids, operands, specs, spec, aliases=aliases
    )


def per_device(inverse_block, factor_column, block_pattern, pivot_inverse):
    levels = lax.axis_size("prow")
    level = lax.axis_index("prow")
    columns = lax.axis_size("pcol")
    column = lax.axis_index("pcol")
    rows = factor_column.shape[0]
    width = factor_column.shape[2] // columns
    per_node = S // width
    blocks = rows // BLK
    node = column // per_node
    ids = jnp.stack([level, column, node]).astype(jnp.int32)

    keep = lax.dynamic_index_in_dim(block_pattern, node, 0, keepdims=False).astype(bf16)
    keep = jnp.broadcast_to(keep[:, None], (blocks, BLK)).reshape(rows, 1, 1)
    own = lax.dynamic_slice_in_dim(factor_column, column * width, width, 2) * keep
    own = own.reshape(rows, 2 * width)
    own, inverse_block = lax.optimization_barrier((own, inverse_block))
    side = lax.dynamic_slice_in_dim(factor_column, node * S, S, 2) * keep
    side = jnp.transpose(side, (1, 2, 0))
    m_pieces, last, (a_across, side) = gather_z(own, (gather_x(inverse_block), side))
    a_pieces = gather_core({0: inverse_block} | a_across)
    total, left = add_products(a_pieces, m_pieces, ids, levels)
    y_parts, p_parts = finish_products(left, last, total, side, ids, levels, columns)

    sums = p_parts[0]
    for d in range(1, levels):
        sums = sums + swap(p_parts[d], "prow", d).astype(f32)
    sums = sums.astype(bf16)
    own_rows = lay_rows(
        [y_parts[0]] + [swap(y_parts[e], "pcol", e) for e in range(1, columns)], ids
    )

    half = levels // 2
    early = [sums] + [swap(sums, "prow", d) for d in range(1, half)]
    late = [swap(sums, "prow", d) for d in range(half, levels)]
    early_across = [gather_x(p) for p in early]
    late, early_across, own_rows = lax.optimization_barrier((late, early_across, own_rows))
    late = [jnp.concatenate(late, 0)]
    late_across = [gather_x(p) for p in late]
    near = [gather_core({0: p}) for p in early + late]
    near = [[g[e] for g in near] for e in range(2)]
    if per_node == 2:
        pivot = take_off(pivot_inverse, near, 0, ids)
        late_across, pivot = lax.optimization_barrier((late_across, pivot))
    there = [gather_core(a) for a in early_across + late_across]
    groups = near + [[g[e] for g in there] for e in range(columns - 2)]
    if per_node != 2:
        pivot = take_off(pivot_inverse, groups[:per_node], 0, ids)
    pivot = take_off(pivot_inverse, groups[per_node:], 1, ids, pivot)
    return own_rows, pivot


def solution(mesh):
    in_specs = (
        P(None, ("pole", "prow"), "pcol"),
        P(("pole", "prow"), None, None),
        P("pole", "prow"),
        P("pole", None, None, None),
    )
    out_specs = (P(("pole", "prow", "pcol"), None, None), P("pole", None, None, None))
    return jax.shard_map(
        per_device, mesh=mesh, in_specs=in_specs, out_specs=out_specs, check_vma=False
    )
```

```python
import functools

import jax
import jax.numpy as jnp
from jax import lax
from jax.experimental import pallas as pl
from jax.experimental.pallas import tpu as pltpu
from jax.sharding import PartitionSpec as P

S = 512
BLK = 128
CHUNKS = 2
COST = 1 << 16
VMEM_LIMIT = 48 * 1024 * 1024
bf16 = jnp.bfloat16
f32 = jnp.float32


def swap(x, axis, distance):
    size = lax.axis_size(axis)
    return lax.ppermute(x, axis, [(i, i ^ distance) for i in range(size)])


def gather_z(chunks, side, beside):
    size = lax.axis_size("prow")
    gathered = []
    for m in chunks:
        pieces = {0: m}
        step = size // 2
        while step > 1:
            pieces |= {d ^ step: swap(p, "prow", step) for d, p in pieces.items()}
            step //= 2
        pieces |= {d ^ 1: swap(p, "prow", 1) for d, p in pieces.items() if d != size - 2}
        gathered.append(pieces)
    last = []
    for n, pieces in enumerate(gathered):
        if n == len(chunks) - 1:
            gathered, beside = lax.optimization_barrier((gathered, beside))
        else:
            far = pieces[size - 2]
            pieces[size - 2], side = lax.optimization_barrier((far, side))
        last.append(swap(gathered[n][size - 2], "prow", 1))
    return gathered, last, side, beside


def gather_x(a):
    size = lax.axis_size("pcol")
    return {e: swap(a, "pcol", e) for e in range(2, size, 2)}


def gather_core(a):
    return [p for e in sorted(a) for p in (a[e], swap(a[e], "pcol", 1))]


def dot(a, b):
    return jnp.dot(a, b, preferred_element_type=f32)


def turn(m):
    width = m.shape[1] // 2
    return jnp.concatenate([-m[:, width:], m[:, :width]], axis=1)


def call(body, out_shape, scalars, operands, specs, out_specs, scratch=(), aliases=None):
    return pl.pallas_call(
        body,
        out_shape=out_shape,
        grid_spec=pltpu.PrefetchScalarGridSpec(
            num_scalar_prefetch=1,
            grid=(1,),
            in_specs=specs,
            out_specs=out_specs,
            scratch_shapes=scratch,
        ),
        input_output_aliases=aliases or {},
        compiler_params=pltpu.CompilerParams(vmem_limit_bytes=VMEM_LIMIT),
        cost_estimate=pl.CostEstimate(flops=0, bytes_accessed=COST, transcendentals=0),
    )(scalars, *operands)


def call_here(body, out_shape, scalars, operands, scratch=()):
    return pl.pallas_call(
        body,
        out_shape=out_shape,
        in_specs=[pl.BlockSpec(memory_space=pltpu.SMEM)]
        + [pl.BlockSpec(memory_space=pltpu.VMEM)] * len(operands),
        out_specs=jax.tree.map(lambda _: pl.BlockSpec(memory_space=pltpu.VMEM), out_shape),
        scratch_shapes=scratch,
        compiler_params=pltpu.CompilerParams(vmem_limit_bytes=VMEM_LIMIT),
        cost_estimate=pl.CostEstimate(flops=0, bytes_accessed=COST, transcendentals=0),
    )(scalars, *operands)


def whole(x):
    return pl.BlockSpec(x.shape, lambda i, ids, n=len(x.shape): (0,) * n)


def add_products(a_pieces, m_chunks, ids, levels):
    rows, wide = m_chunks[0][0].shape
    columns, count = len(a_pieces), len(m_chunks)
    per = levels // columns

    def body(ids_ref, *refs):
        a_refs, refs = refs[:columns], refs[columns:]
        m_refs, refs = refs[: count * (levels - 1)], refs[count * (levels - 1) :]
        total_refs, left_ref, m_all = refs[:count], refs[count], refs[count + 1]
        missing = ids_ref[0] ^ (levels - 1)
        for n, m_ref in enumerate(m_refs):
            m_all[n // (levels - 1), ids_ref[0] ^ (n % (levels - 1))] = m_ref[...]
        for total_ref in total_refs:
            total_ref[...] = jnp.zeros_like(total_ref)
        for e, a_ref in enumerate(a_refs):
            for n in range(per):
                at = (ids_ref[1] ^ e) * per + n
                cut = slice(n * rows, (n + 1) * rows)

                @pl.when(at != missing)
                def _():
                    for c, total_ref in enumerate(total_refs):
                        m = m_all[c, at]
                        total_ref[...] += dot(a_ref[0, :, cut], m) + dot(a_ref[1, :, cut], turn(m))

                @pl.when(at == missing)
                def _():
                    left_ref[...] = a_ref[:, :, cut]

    shapes = [jax.ShapeDtypeStruct((rows, wide), f32)] * count
    shapes += [jax.ShapeDtypeStruct((2, rows, rows), bf16)]
    flat = list(a_pieces) + [chunk[d] for chunk in m_chunks for d in range(levels - 1)]
    out = call_here(
        body,
        shapes,
        ids,
        flat,
        [pltpu.VMEM((count, levels, rows, wide), bf16)],
    )
    return out[:count], out[count]


def finish_products(left, last, total, side, before, ids, levels, columns, final):
    rows, wide = last.shape
    cut = rows // columns
    share = S // levels

    def body(ids_ref, left_ref, m_ref, total_ref, side_ref, *refs):
        before_refs, refs = refs[: len(before)], refs[len(before) :]
        p_out, y_out, y_ref, p_ref = refs[:levels], refs[levels:-2], refs[-2], refs[-1]
        m = m_ref[...]
        y_ref[...] = -(total_ref[...] + dot(left_ref[0], m) + dot(left_ref[1], turn(m)))
        chosen = y_ref[...].astype(bf16)
        p_ref[...] = dot(side_ref[0], chosen) + dot(side_ref[1], turn(chosen))
        for d in range(levels):
            start = pl.multiple_of((ids_ref[0] ^ d) * share, share)
            p_out[d][...] = p_ref[pl.ds(start, share), :].astype(p_out[d].dtype)
        if not final:
            y_out[0][...] = y_ref[...]
            return
        for e in range(columns):
            start = pl.multiple_of((ids_ref[1] ^ e) * cut, cut)
            at = slice(e % 2 * cut, (e % 2 + 1) * cut)
            for n, ref in enumerate(list(before_refs) + [y_ref]):
                value = ref[pl.ds(start, cut), :].astype(y_out[e // 2].dtype)
                y_out[e // 2][at, n * wide : (n + 1) * wide] = value

    shapes = [jax.ShapeDtypeStruct((share, wide), f32 if d == 0 else bf16) for d in range(levels)]
    if final:
        stack = (2 * cut, wide * (1 + len(before)))
        shapes += [jax.ShapeDtypeStruct(stack, bf16 if n else f32) for n in range(columns // 2)]
    else:
        shapes += [jax.ShapeDtypeStruct((rows, wide), f32)]
    operands = [left, last, total, side] + before
    out = call_here(
        body,
        shapes,
        ids,
        operands,
        [pltpu.VMEM((rows, wide), f32), pltpu.VMEM((S, wide), f32)],
    )
    return out[:levels], out[levels:]


def cross_rows(stacks):
    return [stacks[0]] + [swap(y, "pcol", 2 * n) for n, y in enumerate(stacks) if n]


def lay_rows(stacks, chunks, ids):
    columns = len(stacks)
    cut, wide = stacks[0].shape[0] // 2, stacks[0].shape[1]
    width = wide // 2
    some = width // chunks

    def body(ids_ref, *refs):
        for n in range(columns):
            odd = n // (columns // 2)
            e = 2 * (n % (columns // 2)) + odd
            at = slice(odd * cut, (odd + 1) * cut)
            for c in range(chunks):
                for part in range(2):
                    start = pl.multiple_of((ids_ref[1] ^ e) * width + c * some, some)
                    source = (2 * c + part) * some
                    value = refs[n][at, source : source + some].astype(f32)
                    refs[-1][:, part, pl.ds(start, some)] = value

    shape = jax.ShapeDtypeStruct((cut, 2, columns * width), f32)
    return call_here(body, shape, ids, stacks)


def take_off(pivot, stacks, flip, late, levels, ids, rest=None):
    wide = stacks[0].shape[1]
    width = wide // 2
    per_node = S // width
    half = levels // 2
    share = S // levels
    first = per_node * flip

    def body(ids_ref, pivot_ref, *refs):
        for e, ref in enumerate(refs[: len(stacks)]):
            left = pl.multiple_of(((ids_ref[1] ^ (first + e)) % per_node) * width, width)
            for d in range(half):
                top = pl.multiple_of(((ids_ref[0] ^ d) % half) * share, share)
                for part in range(2):
                    at = (0, part, pl.ds(top, share), pl.ds(left, width))
                    piece = ref[d * share : (d + 1) * share, part * width : (part + 1) * width]
                    refs[-1][at] = pivot_ref[at] - piece.astype(f32)

    spec = pl.BlockSpec(
        (1, 2, S // 2, S), lambda i, ids: (ids[2] ^ flip, 0, (ids[0] // half) ^ late, 0)
    )
    operands, specs, aliases = [pivot] + stacks, [spec] + [whole(p) for p in stacks], {}
    if rest is not None:
        operands, specs = operands + [rest], specs + [pl.BlockSpec(memory_space=pl.ANY)]
        aliases = {len(operands): 0}
    return call(
        body, jax.ShapeDtypeStruct(pivot.shape, f32), ids, operands, specs, spec, aliases=aliases
    )


def join(sums):
    some = sums[0].shape[1] // 2
    return jnp.concatenate([s[:, :some] for s in sums] + [s[:, some:] for s in sums], 1)


def per_device(inverse_block, factor_column, block_pattern, pivot_inverse):
    levels = lax.axis_size("prow")
    level = lax.axis_index("prow")
    columns = lax.axis_size("pcol")
    column = lax.axis_index("pcol")
    rows = factor_column.shape[0]
    width = factor_column.shape[2] // columns
    per_node = S // width
    blocks = rows // BLK
    node = column // per_node
    ids = jnp.stack([level, column, node]).astype(jnp.int32)

    chunks = CHUNKS if width % (CHUNKS * 128) == 0 else 1
    some = width // chunks
    raw = lax.dynamic_slice_in_dim(factor_column, column * width, width, 2)
    raw, keep = lax.optimization_barrier(
        (raw, lax.dynamic_index_in_dim(block_pattern, node, 0, keepdims=False))
    )
    keep = jnp.broadcast_to(keep.astype(bf16)[:, None], (blocks, BLK)).reshape(rows, 1)
    own = [raw[:, :, n : n + some].reshape(rows, 2 * some) for n in range(0, width, some)]
    own = [part * keep for part in lax.optimization_barrier(own)]
    keep = keep[:, :, None]
    side = lax.dynamic_slice_in_dim(factor_column, node * S, S, 2) * keep
    side = jnp.transpose(side, (1, 2, 0))
    m_chunks, last, side, a_across = gather_z(own, side, gather_x(inverse_block))
    a_pieces = gather_core({0: inverse_block} | a_across)
    totals, left = add_products(a_pieces, m_chunks, ids, levels)

    before, parts = [], []
    for c in range(chunks):
        p_parts, y_parts = finish_products(
            left, last[c], totals[c], side, before, ids, levels, columns, c == chunks - 1
        )
        before = before + list(y_parts)
        parts.append(p_parts)
    y_stacks = cross_rows(before[chunks - 1 :])

    parts = [
        [p[0]] + [swap(p[d], "prow", d) for d in range(1, levels)] for p in parts
    ]
    parts[-1], y_stacks = lax.optimization_barrier((parts[-1], y_stacks))
    sums = [sum((p.astype(f32) for p in received[1:]), received[0]) for received in parts]
    sums = [total.astype(bf16) for total in sums]

    half = levels // 2
    sums = join(sums)
    pieces = [sums] + [swap(sums, "prow", d) for d in range(1, levels)]
    early = pieces[:half]
    early_across = [gather_x(p) for p in early]
    late, early_across, y_stacks = lax.optimization_barrier(
        (pieces[half:], early_across, y_stacks)
    )
    y_stacks = y_stacks + [swap(y, "pcol", 1) for y in y_stacks]
    own_rows = lay_rows(y_stacks, chunks, ids)
    late = jnp.concatenate(late, 0)
    late_across = gather_x(late)
    early = jnp.concatenate(early, 0)
    early_across = {e: jnp.concatenate([a[e] for a in early_across], 0) for e in late_across}
    take = functools.partial(take_off, pivot_inverse, levels=levels, ids=ids)
    if per_node == 2:
        pivot = take(gather_core({0: early}), 0, 0)
        pivot = take(gather_core({0: late}), 0, 1, rest=pivot)
        pivot = take(gather_core(early_across), 1, 0, rest=pivot)
        late_across, pivot, own_rows = lax.optimization_barrier((late_across, pivot, own_rows))
        pivot = take(gather_core(late_across), 1, 1, rest=pivot)
    else:
        early = gather_core({0: early} | early_across)
        late = gather_core({0: late} | late_across)
        pivot = take(early[:per_node], 0, 0)
        pivot = take(late[:per_node], 0, 1, rest=pivot)
        pivot = take(early[per_node:], 1, 0, rest=pivot)
        pivot = take(late[per_node:], 1, 1, rest=pivot)
    return own_rows, pivot


def solution(mesh):
    in_specs = (
        P(None, ("pole", "prow"), "pcol"),
        P(("pole", "prow"), None, None),
        P("pole", "prow"),
        P("pole", None, None, None),
    )
    out_specs = (P(("pole", "prow", "pcol"), None, None), P("pole", None, None, None))
    return jax.shard_map(
        per_device, mesh=mesh, in_specs=in_specs, out_specs=out_specs, check_vma=False
    )
```

```python
import functools

import jax
import jax.numpy as jnp
from jax import lax
from jax.experimental import pallas as pl
from jax.experimental.pallas import tpu as pltpu
from jax.sharding import PartitionSpec as P

S = 512
BLK = 128
CHUNKS = 2
COST = 1 << 16
VMEM_LIMIT = 48 * 1024 * 1024
bf16 = jnp.bfloat16
f32 = jnp.float32


def swap(x, axis, distance):
    size = lax.axis_size(axis)
    return lax.ppermute(x, axis, [(i, i ^ distance) for i in range(size)])


def gather_z(chunks, side, beside):
    size = lax.axis_size("prow")
    gathered = []
    for m in chunks:
        pieces = {0: m}
        step = size // 2
        while step > 1:
            pieces |= {d ^ step: swap(p, "prow", step) for d, p in pieces.items()}
            step //= 2
        pieces |= {d ^ 1: swap(p, "prow", 1) for d, p in pieces.items() if d != size - 2}
        gathered.append(pieces)
    last = []
    for n, pieces in enumerate(gathered):
        if n == len(chunks) - 1:
            gathered, beside = lax.optimization_barrier((gathered, beside))
        else:
            far = pieces[size - 2]
            pieces[size - 2], side = lax.optimization_barrier((far, side))
        last.append(swap(gathered[n][size - 2], "prow", 1))
    return gathered, last, side, beside


def gather_x(a):
    size = lax.axis_size("pcol")
    return {e: swap(a, "pcol", e) for e in range(2, size, 2)}


def gather_core(a):
    return [p for e in sorted(a) for p in (a[e], swap(a[e], "pcol", 1))]


def dot(a, b):
    return jnp.dot(a, b, preferred_element_type=f32)


def turn(m):
    width = m.shape[1] // 2
    return jnp.concatenate([-m[:, width:], m[:, :width]], axis=1)


def call(body, out_shape, scalars, operands, specs, out_specs, scratch=(), aliases=None, steps=1):
    return pl.pallas_call(
        body,
        out_shape=out_shape,
        grid_spec=pltpu.PrefetchScalarGridSpec(
            num_scalar_prefetch=1,
            grid=(steps,),
            in_specs=specs,
            out_specs=out_specs,
            scratch_shapes=scratch,
        ),
        input_output_aliases=aliases or {},
        compiler_params=pltpu.CompilerParams(vmem_limit_bytes=VMEM_LIMIT),
        cost_estimate=pl.CostEstimate(flops=0, bytes_accessed=COST, transcendentals=0),
    )(scalars, *operands)


def call_here(body, out_shape, scalars, operands, scratch=()):
    return pl.pallas_call(
        body,
        out_shape=out_shape,
        in_specs=[pl.BlockSpec(memory_space=pltpu.SMEM)]
        + [pl.BlockSpec(memory_space=pltpu.VMEM)] * len(operands),
        out_specs=jax.tree.map(lambda _: pl.BlockSpec(memory_space=pltpu.VMEM), out_shape),
        scratch_shapes=scratch,
        compiler_params=pltpu.CompilerParams(vmem_limit_bytes=VMEM_LIMIT),
        cost_estimate=pl.CostEstimate(flops=0, bytes_accessed=COST, transcendentals=0),
    )(scalars, *operands)


def whole(x):
    return pl.BlockSpec(x.shape, lambda i, ids, n=len(x.shape): (0,) * n)


def add_products(a_pieces, m_chunks, ids, levels):
    rows, wide = m_chunks[0][0].shape
    columns, count = len(a_pieces), len(m_chunks)
    per = levels // columns

    def body(ids_ref, *refs):
        a_refs, refs = refs[:columns], refs[columns:]
        m_refs, refs = refs[: count * (levels - 1)], refs[count * (levels - 1) :]
        total_refs, left_ref, m_all = refs[:count], refs[count], refs[count + 1]
        missing = ids_ref[0] ^ (levels - 1)
        for n, m_ref in enumerate(m_refs):
            m_all[n // (levels - 1), ids_ref[0] ^ (n % (levels - 1))] = m_ref[...]
        for total_ref in total_refs:
            total_ref[...] = jnp.zeros_like(total_ref)
        for e, a_ref in enumerate(a_refs):
            for n in range(per):
                at = (ids_ref[1] ^ e) * per + n
                cut = slice(n * rows, (n + 1) * rows)

                @pl.when(at != missing)
                def _():
                    for c, total_ref in enumerate(total_refs):
                        m = m_all[c, at]
                        total_ref[...] += dot(a_ref[0, :, cut], m) + dot(a_ref[1, :, cut], turn(m))

                @pl.when(at == missing)
                def _():
                    left_ref[...] = a_ref[:, :, cut]

    shapes = [jax.ShapeDtypeStruct((rows, wide), f32)] * count
    shapes += [jax.ShapeDtypeStruct((2, rows, rows), bf16)]
    flat = list(a_pieces) + [chunk[d] for chunk in m_chunks for d in range(levels - 1)]
    out = call_here(
        body,
        shapes,
        ids,
        flat,
        [pltpu.VMEM((count, levels, rows, wide), bf16)],
    )
    return out[:count], out[count]


def finish_products(left, last, total, side, before, ids, levels, columns, final):
    rows, wide = last.shape
    cut = rows // columns
    share = S // levels

    def body(ids_ref, left_ref, m_ref, total_ref, side_ref, *refs):
        before_refs, refs = refs[: len(before)], refs[len(before) :]
        p_out, y_out = refs[:levels], refs[levels:-2]
        chosen_ref, turned_ref = refs[-2:]
        m = m_ref[...]
        turned = turn(m)
        for e in range(columns):
            here = pl.ds(pl.multiple_of((ids_ref[1] ^ e) * cut, cut), cut)
            y = -(total_ref[here, :] + dot(left_ref[0, here, :], m) + dot(left_ref[1, here, :], turned))
            chosen = y.astype(bf16)
            chosen_ref[here, :] = chosen
            turned_ref[here, :] = turn(chosen)
            if not final:
                y_out[0][here, :] = y
                continue
            at = slice(e % 2 * cut, (e % 2 + 1) * cut)
            for n, value in enumerate([ref[here, :] for ref in before_refs] + [y]):
                y_out[e // 2][at, n * wide : (n + 1) * wide] = value.astype(y_out[e // 2].dtype)
        chosen, turned = chosen_ref[...], turned_ref[...]
        for d in range(levels):
            here = pl.ds(pl.multiple_of((ids_ref[0] ^ d) * share, share), share)
            part = dot(side_ref[0, here, :], chosen) + dot(side_ref[1, here, :], turned)
            p_out[d][...] = part.astype(p_out[d].dtype)

    shapes = [jax.ShapeDtypeStruct((share, wide), f32 if d == 0 else bf16) for d in range(levels)]
    if final:
        stack = (2 * cut, wide * (1 + len(before)))
        shapes += [jax.ShapeDtypeStruct(stack, bf16 if n else f32) for n in range(columns // 2)]
    else:
        shapes += [jax.ShapeDtypeStruct((rows, wide), f32)]
    operands = [left, last, total, side] + before
    out = call_here(
        body,
        shapes,
        ids,
        operands,
        [pltpu.VMEM((rows, wide), bf16)] * 2,
    )
    return out[:levels], out[levels:]


def cross_rows(stacks):
    return [stacks[0]] + [swap(y, "pcol", 2 * n) for n, y in enumerate(stacks) if n]


def lay_rows(stacks, chunks, ids):
    columns = len(stacks)
    cut, wide = stacks[0].shape[0] // 2, stacks[0].shape[1]
    width = wide // 2
    some = width // chunks

    def body(ids_ref, *refs):
        for n in range(columns):
            odd = n // (columns // 2)
            e = 2 * (n % (columns // 2)) + odd
            at = slice(odd * cut, (odd + 1) * cut)
            for c in range(chunks):
                for part in range(2):
                    start = pl.multiple_of((ids_ref[1] ^ e) * width + c * some, some)
                    source = (2 * c + part) * some
                    value = refs[n][at, source : source + some].astype(f32)
                    refs[-1][:, part, pl.ds(start, some)] = value

    shape = jax.ShapeDtypeStruct((cut, 2, columns * width), f32)
    return call_here(body, shape, ids, stacks)


def take_off(pivot, jobs, levels, ids, rest=None):
    stacks = [p for _, _, groups in jobs for group in groups for p in group]
    wide = stacks[0].shape[1]
    width = wide // 2
    per_node = S // width
    part_levels = levels // 2
    share = S // levels

    def body(ids_ref, pivot_ref, *refs):
        out_ref, refs = refs[-1], list(refs)
        for job, (flip, half, groups) in enumerate(jobs):
            mine = [[(refs.pop(0), p.shape[0]) for p in group] for group in groups]

            @pl.when(pl.program_id(0) == job)
            def _():
                base = ((ids_ref[0] // part_levels) ^ half) * (S // 2)
                for e, group in enumerate(mine):
                    left = pl.multiple_of(((ids_ref[1] ^ e) % per_node) * width, width)
                    d = 0
                    for ref, height in group:
                        for row in range(0, height, share):
                            top = pl.multiple_of(((ids_ref[0] ^ d) % part_levels) * share, share)
                            source = pl.multiple_of(base + top, share)
                            for part in range(2):
                                piece = ref[row : row + share, part * width : (part + 1) * width]
                                old = pivot_ref[
                                    ids_ref[2] ^ flip, part, pl.ds(source, share), pl.ds(left, width)
                                ]
                                out_ref[0, part, pl.ds(top, share), pl.ds(left, width)] = (
                                    old - piece.astype(f32)
                                )
                            d += 1

    def place(i, ids):
        flip, half = jobs[-1][0], jobs[-1][1]
        for job in range(len(jobs) - 1):
            flip = jnp.where(i == job, jobs[job][0], flip)
            half = jnp.where(i == job, jobs[job][1], half)
        return ids[2] ^ flip, 0, (ids[0] // part_levels) ^ half, 0

    spec = pl.BlockSpec((1, 2, S // 2, S), place)
    operands, aliases = [pivot] + stacks, {}
    specs = [pl.BlockSpec(memory_space=pltpu.VMEM)] * len(operands)
    if rest is not None:
        operands, specs = operands + [rest], specs + [pl.BlockSpec(memory_space=pl.ANY)]
        aliases = {len(operands): 0}
    shape = jax.ShapeDtypeStruct(pivot.shape, f32)
    return call(body, shape, ids, operands, specs, spec, aliases=aliases, steps=len(jobs))


def join(sums):
    some = sums[0].shape[1] // 2
    return jnp.concatenate([s[:, :some] for s in sums] + [s[:, some:] for s in sums], 1)


def per_device(inverse_block, factor_column, block_pattern, pivot_inverse):
    levels = lax.axis_size("prow")
    level = lax.axis_index("prow")
    columns = lax.axis_size("pcol")
    column = lax.axis_index("pcol")
    rows = factor_column.shape[0]
    width = factor_column.shape[2] // columns
    per_node = S // width
    blocks = rows // BLK
    node = column // per_node
    ids = jnp.stack([level, column, node]).astype(jnp.int32)

    chunks = CHUNKS if width % (CHUNKS * 128) == 0 else 1
    some = width // chunks
    raw = lax.dynamic_slice_in_dim(factor_column, column * width, width, 2)
    raw, keep = lax.optimization_barrier(
        (raw, lax.dynamic_index_in_dim(block_pattern, node, 0, keepdims=False))
    )
    keep = jnp.broadcast_to(keep.astype(bf16)[:, None], (blocks, BLK)).reshape(rows, 1)
    own = [raw[:, :, n : n + some].reshape(rows, 2 * some) for n in range(0, width, some)]
    own = [part * keep for part in lax.optimization_barrier(own)]
    keep = keep[:, :, None]
    side = lax.dynamic_slice_in_dim(factor_column, node * S, S, 2) * keep
    side = jnp.transpose(side, (1, 2, 0))
    m_chunks, last, side, a_across = gather_z(own, side, gather_x(inverse_block))
    a_pieces = gather_core({0: inverse_block} | a_across)
    totals, left = add_products(a_pieces, m_chunks, ids, levels)

    before, parts = [], []
    for c in range(chunks):
        p_parts, y_parts = finish_products(
            left, last[c], totals[c], side, before, ids, levels, columns, c == chunks - 1
        )
        before = before + list(y_parts)
        parts.append(p_parts)
    y_stacks = cross_rows(before[chunks - 1 :])

    parts = [
        [p[0]] + [swap(p[d], "prow", d) for d in range(1, levels)] for p in parts
    ]
    sums = []
    for received in parts:
        if len(sums) == chunks - 1:
            received, y_stacks = lax.optimization_barrier((received, y_stacks))
        sums, received = lax.optimization_barrier((sums, received))
        total = sum((p.astype(f32) for p in received[1:]), received[0])
        sums = sums + [total.astype(bf16)]

    half = levels // 2
    sums = join(sums)
    pieces = [sums] + [swap(sums, "prow", d) for d in range(1, levels)]
    early = pieces[:half]
    early_across = [gather_x(p) for p in early]
    late, early_across, y_stacks = lax.optimization_barrier(
        (pieces[half:], early_across, y_stacks)
    )
    y_stacks = y_stacks + [swap(y, "pcol", 1) for y in y_stacks]
    own_rows = lay_rows(y_stacks, chunks, ids)
    late = jnp.concatenate(late, 0)
    late_across = gather_x(late)
    early = jnp.concatenate(early, 0)
    early_across = {e: jnp.concatenate([a[e] for a in early_across], 0) for e in late_across}
    take = functools.partial(take_off, pivot_inverse, levels=levels, ids=ids)
    one = lambda stacks: [[p] for p in stacks]
    if per_node == 2:
        pivot = take([(0, 0, one(gather_core({0: early}))), (1, 0, one(gather_core(early_across)))])
        pivot = take([(0, 1, one(gather_core({0: late})))], rest=pivot)
        late_across, pivot, own_rows = lax.optimization_barrier((late_across, pivot, own_rows))
        pivot = take([(1, 1, one(gather_core(late_across)))], rest=pivot)
    else:
        early = one(gather_core({0: early} | early_across))
        late = one(gather_core({0: late} | late_across))
        pivot = take(
            [
                (flip, half, part[flip * per_node : (flip + 1) * per_node])
                for flip in range(2)
                for half, part in enumerate((early, late))
            ]
        )
    return own_rows, pivot


def solution(mesh):
    in_specs = (
        P(None, ("pole", "prow"), "pcol"),
        P(("pole", "prow"), None, None),
        P("pole", "prow"),
        P("pole", None, None, None),
    )
    out_specs = (P(("pole", "prow", "pcol"), None, None), P("pole", None, None, None))
    return jax.shard_map(
        per_device, mesh=mesh, in_specs=in_specs, out_specs=out_specs, check_vma=False
    )
```

```python
import functools

import jax
import jax.numpy as jnp
from jax import lax
from jax.experimental import pallas as pl
from jax.experimental.pallas import tpu as pltpu
from jax.sharding import PartitionSpec as P

S = 512
BLK = 128
CHUNKS = 2
COST = 1 << 16
VMEM_LIMIT = 48 * 1024 * 1024
bf16 = jnp.bfloat16
f32 = jnp.float32


def swap(x, axis, distance):
    size = lax.axis_size(axis)
    return lax.ppermute(x, axis, [(i, i ^ distance) for i in range(size)])


def gather_z(chunks, side, beside):
    size = lax.axis_size("prow")
    gathered = []
    for m in chunks:
        pieces = {0: m}
        step = size // 2
        while step > 1:
            pieces |= {d ^ step: swap(p, "prow", step) for d, p in pieces.items()}
            step //= 2
        pieces |= {d ^ 1: swap(p, "prow", 1) for d, p in pieces.items() if d != size - 2}
        gathered.append(pieces)
    last = []
    for n, pieces in enumerate(gathered):
        if n == len(chunks) - 1:
            gathered, beside = lax.optimization_barrier((gathered, beside))
        else:
            far = pieces[size - 2]
            pieces[size - 2], side = lax.optimization_barrier((far, side))
        last.append(swap(gathered[n][size - 2], "prow", 1))
    return gathered, last, side, beside


def gather_x(a):
    size = lax.axis_size("pcol")
    return {e: swap(a, "pcol", e) for e in range(2, size, 2)}


def gather_core(a):
    return [p for e in sorted(a) for p in (a[e], swap(a[e], "pcol", 1))]


def dot(a, b):
    return jnp.dot(a, b, preferred_element_type=f32)


def turn(m):
    width = m.shape[1] // 2
    return jnp.concatenate([-m[:, width:], m[:, :width]], axis=1)


def call(body, out_shape, scalars, operands, specs, out_specs, scratch=(), aliases=None, steps=1):
    return pl.pallas_call(
        body,
        out_shape=out_shape,
        grid_spec=pltpu.PrefetchScalarGridSpec(
            num_scalar_prefetch=1,
            grid=(steps,),
            in_specs=specs,
            out_specs=out_specs,
            scratch_shapes=scratch,
        ),
        input_output_aliases=aliases or {},
        compiler_params=pltpu.CompilerParams(vmem_limit_bytes=VMEM_LIMIT),
        cost_estimate=pl.CostEstimate(flops=0, bytes_accessed=COST, transcendentals=0),
    )(scalars, *operands)


def call_here(body, out_shape, scalars, operands, scratch=()):
    return pl.pallas_call(
        body,
        out_shape=out_shape,
        in_specs=[pl.BlockSpec(memory_space=pltpu.SMEM)]
        + [pl.BlockSpec(memory_space=pltpu.VMEM)] * len(operands),
        out_specs=jax.tree.map(lambda _: pl.BlockSpec(memory_space=pltpu.VMEM), out_shape),
        scratch_shapes=scratch,
        compiler_params=pltpu.CompilerParams(vmem_limit_bytes=VMEM_LIMIT),
        cost_estimate=pl.CostEstimate(flops=0, bytes_accessed=COST, transcendentals=0),
    )(scalars, *operands)


def whole(x):
    return pl.BlockSpec(x.shape, lambda i, ids, n=len(x.shape): (0,) * n)


def add_products(a_pieces, m_chunks, ids, levels):
    rows, wide = m_chunks[0][0].shape
    columns, count = len(a_pieces), len(m_chunks)
    per = levels // columns

    def body(ids_ref, *refs):
        a_refs, refs = refs[:columns], refs[columns:]
        m_refs, refs = refs[: count * (levels - 1)], refs[count * (levels - 1) :]
        total_refs, left_ref, m_all = refs[:count], refs[count], refs[count + 1]
        missing = ids_ref[0] ^ (levels - 1)
        for n, m_ref in enumerate(m_refs):
            m_all[n // (levels - 1), ids_ref[0] ^ (n % (levels - 1))] = m_ref[...]
        for total_ref in total_refs:
            total_ref[...] = jnp.zeros_like(total_ref)
        for e, a_ref in enumerate(a_refs):
            for n in range(per):
                at = (ids_ref[1] ^ e) * per + n
                cut = slice(n * rows, (n + 1) * rows)

                @pl.when(at != missing)
                def _():
                    for c, total_ref in enumerate(total_refs):
                        m = m_all[c, at]
                        total_ref[...] += dot(a_ref[0, :, cut], m) + dot(a_ref[1, :, cut], turn(m))

                @pl.when(at == missing)
                def _():
                    left_ref[...] = a_ref[:, :, cut]

    shapes = [jax.ShapeDtypeStruct((rows, wide), f32)] * count
    shapes += [jax.ShapeDtypeStruct((2, rows, rows), bf16)]
    flat = list(a_pieces) + [chunk[d] for chunk in m_chunks for d in range(levels - 1)]
    out = call_here(
        body,
        shapes,
        ids,
        flat,
        [pltpu.VMEM((count, levels, rows, wide), bf16)],
    )
    return out[:count], out[count]


def finish_products(left, last, total, side, before, ids, levels, columns, final):
    rows, wide = last.shape
    cut = rows // columns
    share = S // levels

    def body(ids_ref, left_ref, m_ref, total_ref, side_ref, *refs):
        before_refs, refs = refs[: len(before)], refs[len(before) :]
        p_out, y_out = refs[:levels], refs[levels:-3]
        chosen_ref, turned_ref, y_all = refs[-3:]
        m = m_ref[...]
        turned = turn(m)
        tile = rows // 2
        for top in range(0, rows, tile):
            here = slice(top, top + tile)
            y = -(total_ref[here, :] + dot(left_ref[0, here, :], m) + dot(left_ref[1, here, :], turned))
            (y_all if final else y_out[0])[here, :] = y
            chosen_ref[here, :] = y.astype(bf16)
            turned_ref[here, :] = turn(y.astype(bf16))
        chosen, turned = chosen_ref[...], turned_ref[...]
        for d in range(levels):
            here = pl.ds(pl.multiple_of((ids_ref[0] ^ d) * share, share), share)
            part = dot(side_ref[0, here, :], chosen) + dot(side_ref[1, here, :], turned)
            p_out[d][...] = part.astype(p_out[d].dtype)

        if not final:
            return
        for e in range(columns):
            here = pl.ds(pl.multiple_of((ids_ref[1] ^ e) * cut, cut), cut)
            at = slice(e % 2 * cut, (e % 2 + 1) * cut)
            for n, ref in enumerate(list(before_refs) + [y_all]):
                y_out[e // 2][at, n * wide : (n + 1) * wide] = ref[here, :].astype(y_out[e // 2].dtype)

    shapes = [jax.ShapeDtypeStruct((share, wide), f32 if d == 0 else bf16) for d in range(levels)]
    if final:
        stack = (2 * cut, wide * (1 + len(before)))
        shapes += [jax.ShapeDtypeStruct(stack, bf16 if n else f32) for n in range(columns // 2)]
    else:
        shapes += [jax.ShapeDtypeStruct((rows, wide), f32)]
    operands = [left, last, total, side] + before
    out = call_here(
        body,
        shapes,
        ids,
        operands,
        [pltpu.VMEM((rows, wide), bf16)] * 2 + [pltpu.VMEM((rows, wide), f32)],
    )
    return out[:levels], out[levels:]


def cross_rows(stacks):
    return [stacks[0]] + [swap(y, "pcol", 2 * n) for n, y in enumerate(stacks) if n]


def lay_rows(stacks, chunks, ids):
    columns = len(stacks)
    cut, wide = stacks[0].shape[0] // 2, stacks[0].shape[1]
    width = wide // 2
    some = width // chunks

    def body(ids_ref, *refs):
        for n in range(columns):
            odd = n // (columns // 2)
            e = 2 * (n % (columns // 2)) + odd
            at = slice(odd * cut, (odd + 1) * cut)
            for c in range(chunks):
                for part in range(2):
                    start = pl.multiple_of((ids_ref[1] ^ e) * width + c * some, some)
                    source = (2 * c + part) * some
                    value = refs[n][at, source : source + some].astype(f32)
                    refs[-1][:, part, pl.ds(start, some)] = value

    shape = jax.ShapeDtypeStruct((cut, 2, columns * width), f32)
    return call_here(body, shape, ids, stacks)


def take_off(pivot, jobs, levels, ids, rest=None):
    stacks = [p for _, _, groups in jobs for group in groups for p in group]
    wide = stacks[0].shape[1]
    width = wide // 2
    per_node = S // width
    part_levels = levels // 2
    share = S // levels

    def body(ids_ref, pivot_ref, *refs):
        out_ref, refs = refs[-1], list(refs)
        for job, (flip, half, groups) in enumerate(jobs):
            mine = [[(refs.pop(0), p.shape[0]) for p in group] for group in groups]

            @pl.when(pl.program_id(0) // 2 == job)
            def _():
                part = pl.program_id(0) % 2
                base = ((ids_ref[0] // part_levels) ^ half) * (S // 2)
                for e, group in enumerate(mine):
                    left = pl.multiple_of(((ids_ref[1] ^ e) % per_node) * width, width)
                    d = 0
                    for ref, height in group:
                        for row in range(0, height, share):
                            top = pl.multiple_of(((ids_ref[0] ^ d) % part_levels) * share, share)
                            source = pl.multiple_of(base + top, share)
                            piece = jnp.where(
                                part == 0,
                                ref[row : row + share, :width],
                                ref[row : row + share, width:],
                            )
                            old = pivot_ref[
                                ids_ref[2] ^ flip, part, pl.ds(source, share), pl.ds(left, width)
                            ]
                            out_ref[0, 0, pl.ds(top, share), pl.ds(left, width)] = (
                                old - piece.astype(f32)
                            )
                            d += 1

    def place(i, ids):
        flip, half = jobs[-1][0], jobs[-1][1]
        for job in range(len(jobs) - 1):
            flip = jnp.where(i // 2 == job, jobs[job][0], flip)
            half = jnp.where(i // 2 == job, jobs[job][1], half)
        return ids[2] ^ flip, i % 2, (ids[0] // part_levels) ^ half, 0

    spec = pl.BlockSpec((1, 1, S // 2, S), place)
    operands, aliases = [pivot] + stacks, {}
    specs = [pl.BlockSpec(memory_space=pltpu.VMEM)] * len(operands)
    if rest is not None:
        operands, specs = operands + [rest], specs + [pl.BlockSpec(memory_space=pl.ANY)]
        aliases = {len(operands): 0}
    shape = jax.ShapeDtypeStruct(pivot.shape, f32)
    return call(body, shape, ids, operands, specs, spec, aliases=aliases, steps=2 * len(jobs))


def join(sums):
    some = sums[0].shape[1] // 2
    return jnp.concatenate([s[:, :some] for s in sums] + [s[:, some:] for s in sums], 1)


def per_device(inverse_block, factor_column, block_pattern, pivot_inverse):
    levels = lax.axis_size("prow")
    level = lax.axis_index("prow")
    columns = lax.axis_size("pcol")
    column = lax.axis_index("pcol")
    rows = factor_column.shape[0]
    width = factor_column.shape[2] // columns
    per_node = S // width
    blocks = rows // BLK
    node = column // per_node
    ids = jnp.stack([level, column, node]).astype(jnp.int32)

    chunks = CHUNKS if width % (CHUNKS * 128) == 0 else 1
    some = width // chunks
    raw = lax.dynamic_slice_in_dim(factor_column, column * width, width, 2)
    raw, keep = lax.optimization_barrier(
        (raw, lax.dynamic_index_in_dim(block_pattern, node, 0, keepdims=False))
    )
    keep = jnp.broadcast_to(keep.astype(bf16)[:, None], (blocks, BLK)).reshape(rows, 1)
    own = [raw[:, :, n : n + some].reshape(rows, 2 * some) for n in range(0, width, some)]
    own = [part * keep for part in lax.optimization_barrier(own)]
    keep = keep[:, :, None]
    side = lax.dynamic_slice_in_dim(factor_column, node * S, S, 2) * keep
    side = jnp.transpose(side, (1, 2, 0))
    m_chunks, last, side, a_across = gather_z(own, side, gather_x(inverse_block))
    a_pieces = gather_core({0: inverse_block} | a_across)
    totals, left = add_products(a_pieces, m_chunks, ids, levels)

    before, parts = [], []
    for c in range(chunks):
        p_parts, y_parts = finish_products(
            left, last[c], totals[c], side, before, ids, levels, columns, c == chunks - 1
        )
        before = before + list(y_parts)
        parts.append(p_parts)
    y_stacks = cross_rows(before[chunks - 1 :])

    parts = [
        [p[0]] + [swap(p[d], "prow", d) for d in range(1, levels)] for p in parts
    ]
    sums = []
    for received in parts:
        if len(sums) == chunks - 1:
            received, y_stacks = lax.optimization_barrier((received, y_stacks))
        sums, received = lax.optimization_barrier((sums, received))
        total = sum((p.astype(f32) for p in received[1:]), received[0])
        sums = sums + [total.astype(bf16)]

    half = levels // 2
    sums = join(sums)
    pieces = [sums] + [swap(sums, "prow", d) for d in range(1, levels)]
    early = pieces[:half]
    early_across = [gather_x(p) for p in early]
    late, early_across, y_stacks = lax.optimization_barrier(
        (pieces[half:], early_across, y_stacks)
    )
    y_stacks = y_stacks + [swap(y, "pcol", 1) for y in y_stacks]
    own_rows = lay_rows(y_stacks, chunks, ids)
    late = jnp.concatenate(late, 0)
    late_across = gather_x(late)
    early = jnp.concatenate(early, 0)
    early_across = {e: jnp.concatenate([a[e] for a in early_across], 0) for e in late_across}
    take = functools.partial(take_off, pivot_inverse, levels=levels, ids=ids)
    one = lambda stacks: [[p] for p in stacks]
    if per_node == 2:
        pivot = take([(0, 0, one(gather_core({0: early}))), (1, 0, one(gather_core(early_across)))])
        pivot = take([(0, 1, one(gather_core({0: late})))], rest=pivot)
        late_across, pivot, own_rows = lax.optimization_barrier((late_across, pivot, own_rows))
        pivot = take([(1, 1, one(gather_core(late_across)))], rest=pivot)
    else:
        early = one(gather_core({0: early} | early_across))
        late = one(gather_core({0: late} | late_across))
        pivot = take(
            [
                (flip, half, part[flip * per_node : (flip + 1) * per_node])
                for flip in range(2)
                for half, part in enumerate((early, late))
            ]
        )
    return own_rows, pivot


def solution(mesh):
    in_specs = (
        P(None, ("pole", "prow"), "pcol"),
        P(("pole", "prow"), None, None),
        P("pole", "prow"),
        P("pole", None, None, None),
    )
    out_specs = (P(("pole", "prow", "pcol"), None, None), P("pole", None, None, None))
    return jax.shard_map(
        per_device, mesh=mesh, in_specs=in_specs, out_specs=out_specs, check_vma=False
    )
```

```python
import functools

import jax
import jax.numpy as jnp
from jax import lax
from jax.experimental import pallas as pl
from jax.experimental.pallas import tpu as pltpu
from jax.sharding import PartitionSpec as P

S = 512
BLK = 128
CHUNKS = 2
COST = 1 << 16
VMEM_ROOM = 8 * 1024 * 1024
bf16 = jnp.bfloat16
f32 = jnp.float32


def swap(x, axis, distance):
    size = lax.axis_size(axis)
    return lax.ppermute(x, axis, [(i, i ^ distance) for i in range(size)])


def gather_z(chunks, side, beside):
    size = lax.axis_size("prow")
    gathered = []
    for m in chunks:
        pieces = {0: m}
        step = size // 2
        while step > 1:
            pieces |= {d ^ step: swap(p, "prow", step) for d, p in pieces.items()}
            step //= 2
        pieces |= {d ^ 1: swap(p, "prow", 1) for d, p in pieces.items() if d != size - 2}
        gathered.append(pieces)
    last = []
    for n, pieces in enumerate(gathered):
        if n == len(chunks) - 1:
            gathered, beside = lax.optimization_barrier((gathered, beside))
        else:
            far = pieces[size - 2]
            pieces[size - 2], side = lax.optimization_barrier((far, side))
        last.append(swap(gathered[n][size - 2], "prow", 1))
    return gathered, last, side, beside


def gather_x(a):
    size = lax.axis_size("pcol")
    return {e: swap(a, "pcol", e) for e in range(2, size, 2)}


def gather_core(a):
    return [p for e in sorted(a) for p in (a[e], swap(a[e], "pcol", 1))]


def dot(a, b):
    return jnp.dot(a, b, preferred_element_type=f32)


def turn(m):
    width = m.shape[1] // 2
    return jnp.concatenate([-m[:, width:], m[:, :width]], axis=1)


def held(arrays):
    return sum(x.size * x.dtype.itemsize for x in arrays)


def call(body, out_shape, scalars, operands, specs, out_specs, scratch=(), aliases=None, steps=1):
    return pl.pallas_call(
        body,
        out_shape=out_shape,
        grid_spec=pltpu.PrefetchScalarGridSpec(
            num_scalar_prefetch=1,
            grid=(steps,),
            in_specs=specs,
            out_specs=out_specs,
            scratch_shapes=scratch,
        ),
        input_output_aliases=aliases or {},
        compiler_params=pltpu.CompilerParams(vmem_limit_bytes=VMEM_ROOM + held(operands)),
        cost_estimate=pl.CostEstimate(flops=0, bytes_accessed=COST, transcendentals=0),
    )(scalars, *operands)


def call_here(body, out_shape, scalars, operands, scratch=()):
    return pl.pallas_call(
        body,
        out_shape=out_shape,
        in_specs=[pl.BlockSpec(memory_space=pltpu.SMEM)]
        + [pl.BlockSpec(memory_space=pltpu.VMEM)] * len(operands),
        out_specs=jax.tree.map(lambda _: pl.BlockSpec(memory_space=pltpu.VMEM), out_shape),
        scratch_shapes=scratch,
        compiler_params=pltpu.CompilerParams(vmem_limit_bytes=VMEM_ROOM + held(operands)),
        cost_estimate=pl.CostEstimate(flops=0, bytes_accessed=COST, transcendentals=0),
    )(scalars, *operands)


def whole(x):
    return pl.BlockSpec(x.shape, lambda i, ids, n=len(x.shape): (0,) * n)


def add_products(a_pieces, m_chunks, ids, levels):
    rows, wide = m_chunks[0][0].shape
    columns, count = len(a_pieces), len(m_chunks)
    per = levels // columns

    def body(ids_ref, *refs):
        a_refs, refs = refs[:columns], refs[columns:]
        m_refs, refs = refs[: count * (levels - 1)], refs[count * (levels - 1) :]
        total_refs, left_ref, m_all = refs[:count], refs[count], refs[count + 1]
        missing = ids_ref[0] ^ (levels - 1)
        for n, m_ref in enumerate(m_refs):
            m_all[n // (levels - 1), ids_ref[0] ^ (n % (levels - 1))] = m_ref[...]
        for total_ref in total_refs:
            total_ref[...] = jnp.zeros_like(total_ref)
        for e, a_ref in enumerate(a_refs):
            for n in range(per):
                at = (ids_ref[1] ^ e) * per + n
                cut = slice(n * rows, (n + 1) * rows)

                @pl.when(at != missing)
                def _():
                    for c, total_ref in enumerate(total_refs):
                        m = m_all[c, at]
                        total_ref[...] += dot(a_ref[0, :, cut], m) + dot(a_ref[1, :, cut], turn(m))

                @pl.when(at == missing)
                def _():
                    left_ref[...] = a_ref[:, :, cut]

    shapes = [jax.ShapeDtypeStruct((rows, wide), f32)] * count
    shapes += [jax.ShapeDtypeStruct((2, rows, rows), bf16)]
    flat = list(a_pieces) + [chunk[d] for chunk in m_chunks for d in range(levels - 1)]
    out = call_here(
        body,
        shapes,
        ids,
        flat,
        [pltpu.VMEM((count, levels, rows, wide), bf16)],
    )
    return out[:count], out[count]


def finish_products(left, last, total, side, before, ids, levels, columns, final):
    rows, wide = last.shape
    cut = rows // columns
    share = S // levels

    def body(ids_ref, left_ref, m_ref, total_ref, side_ref, *refs):
        before_refs, refs = refs[: len(before)], refs[len(before) :]
        p_out, y_out = refs[:levels], refs[levels:-3]
        chosen_ref, turned_ref, y_all = refs[-3:]
        m = m_ref[...]
        turned = turn(m)
        tile = rows // 2
        for top in range(0, rows, tile):
            here = slice(top, top + tile)
            y = -(total_ref[here, :] + dot(left_ref[0, here, :], m) + dot(left_ref[1, here, :], turned))
            (y_all if final else y_out[0])[here, :] = y
            chosen_ref[here, :] = y.astype(bf16)
            turned_ref[here, :] = turn(y.astype(bf16))
        chosen, turned = chosen_ref[...], turned_ref[...]
        for d in range(levels):
            here = pl.ds(pl.multiple_of((ids_ref[0] ^ d) * share, share), share)
            part = dot(side_ref[0, here, :], chosen) + dot(side_ref[1, here, :], turned)
            p_out[d][...] = part.astype(p_out[d].dtype)

        if not final:
            return
        for e in range(columns):
            here = pl.ds(pl.multiple_of((ids_ref[1] ^ e) * cut, cut), cut)
            at = slice(e % 2 * cut, (e % 2 + 1) * cut)
            for n, ref in enumerate(list(before_refs) + [y_all]):
                y_out[e // 2][at, n * wide : (n + 1) * wide] = ref[here, :].astype(y_out[e // 2].dtype)

    shapes = [jax.ShapeDtypeStruct((share, wide), f32 if d == 0 else bf16) for d in range(levels)]
    if final:
        stack = (2 * cut, wide * (1 + len(before)))
        shapes += [jax.ShapeDtypeStruct(stack, bf16 if n else f32) for n in range(columns // 2)]
    else:
        shapes += [jax.ShapeDtypeStruct((rows, wide), f32)]
    operands = [left, last, total, side] + before
    out = call_here(
        body,
        shapes,
        ids,
        operands,
        [pltpu.VMEM((rows, wide), bf16)] * 2 + [pltpu.VMEM((rows, wide), f32)],
    )
    return out[:levels], out[levels:]


def cross_rows(stacks):
    return [stacks[0]] + [swap(y, "pcol", 2 * n) for n, y in enumerate(stacks) if n]


def lay_rows(stacks, chunks, ids):
    columns = len(stacks)
    cut, wide = stacks[0].shape[0] // 2, stacks[0].shape[1]
    width = wide // 2
    some = width // chunks

    def body(ids_ref, *refs):
        for n in range(columns):
            odd = n // (columns // 2)
            e = 2 * (n % (columns // 2)) + odd
            at = slice(odd * cut, (odd + 1) * cut)
            for c in range(chunks):
                for part in range(2):
                    start = pl.multiple_of((ids_ref[1] ^ e) * width + c * some, some)
                    source = (2 * c + part) * some
                    value = refs[n][at, source : source + some].astype(f32)
                    refs[-1][:, part, pl.ds(start, some)] = value

    shape = jax.ShapeDtypeStruct((cut, 2, columns * width), f32)
    return call_here(body, shape, ids, stacks)


def take_off(pivot, jobs, levels, ids, rest=None):
    stacks = [p for _, _, groups in jobs for group in groups for p in group]
    wide = stacks[0].shape[1]
    width = wide // 2
    per_node = S // width
    part_levels = levels // 2
    share = S // levels

    def body(ids_ref, pivot_ref, *refs):
        out_ref, refs = refs[-1], list(refs)
        for job, (flip, half, groups) in enumerate(jobs):
            mine = [[(refs.pop(0), p.shape[0]) for p in group] for group in groups]

            @pl.when(pl.program_id(0) // 2 == job)
            def _():
                part = pl.program_id(0) % 2
                base = ((ids_ref[0] // part_levels) ^ half) * (S // 2)
                for e, group in enumerate(mine):
                    left = pl.multiple_of(((ids_ref[1] ^ e) % per_node) * width, width)
                    d = 0
                    for ref, height in group:
                        for row in range(0, height, share):
                            top = pl.multiple_of(((ids_ref[0] ^ d) % part_levels) * share, share)
                            source = pl.multiple_of(base + top, share)
                            piece = jnp.where(
                                part == 0,
                                ref[row : row + share, :width],
                                ref[row : row + share, width:],
                            )
                            old = pivot_ref[
                                ids_ref[2] ^ flip, part, pl.ds(source, share), pl.ds(left, width)
                            ]
                            out_ref[0, 0, pl.ds(top, share), pl.ds(left, width)] = (
                                old - piece.astype(f32)
                            )
                            d += 1

    def place(i, ids):
        flip, half = jobs[-1][0], jobs[-1][1]
        for job in range(len(jobs) - 1):
            flip = jnp.where(i // 2 == job, jobs[job][0], flip)
            half = jnp.where(i // 2 == job, jobs[job][1], half)
        return ids[2] ^ flip, i % 2, (ids[0] // part_levels) ^ half, 0

    spec = pl.BlockSpec((1, 1, S // 2, S), place)
    operands, aliases = [pivot] + stacks, {}
    specs = [pl.BlockSpec(memory_space=pltpu.VMEM)] * len(operands)
    if rest is not None:
        operands, specs = operands + [rest], specs + [pl.BlockSpec(memory_space=pl.ANY)]
        aliases = {len(operands): 0}
    shape = jax.ShapeDtypeStruct(pivot.shape, f32)
    return call(body, shape, ids, operands, specs, spec, aliases=aliases, steps=2 * len(jobs))


def join(sums):
    some = sums[0].shape[1] // 2
    return jnp.concatenate([s[:, :some] for s in sums] + [s[:, some:] for s in sums], 1)


def per_device(inverse_block, factor_column, block_pattern, pivot_inverse):
    levels = lax.axis_size("prow")
    level = lax.axis_index("prow")
    columns = lax.axis_size("pcol")
    column = lax.axis_index("pcol")
    rows = factor_column.shape[0]
    width = factor_column.shape[2] // columns
    per_node = S // width
    blocks = rows // BLK
    node = column // per_node
    ids = jnp.stack([level, column, node]).astype(jnp.int32)

    chunks = CHUNKS if width % (CHUNKS * 128) == 0 else 1
    some = width // chunks
    raw = lax.dynamic_slice_in_dim(factor_column, column * width, width, 2)
    raw, keep = lax.optimization_barrier(
        (raw, lax.dynamic_index_in_dim(block_pattern, node, 0, keepdims=False))
    )
    keep = jnp.broadcast_to(keep.astype(bf16)[:, None], (blocks, BLK)).reshape(rows, 1)
    own = [raw[:, :, n : n + some].reshape(rows, 2 * some) for n in range(0, width, some)]
    own = [part * keep for part in lax.optimization_barrier(own)]
    keep = keep[:, :, None]
    side = lax.dynamic_slice_in_dim(factor_column, node * S, S, 2) * keep
    side = jnp.transpose(side, (1, 2, 0))
    m_chunks, last, side, a_across = gather_z(own, side, gather_x(inverse_block))
    a_pieces = gather_core({0: inverse_block} | a_across)
    totals, left = add_products(a_pieces, m_chunks, ids, levels)

    before, parts = [], []
    for c in range(chunks):
        p_parts, y_parts = finish_products(
            left, last[c], totals[c], side, before, ids, levels, columns, c == chunks - 1
        )
        before = before + list(y_parts)
        parts.append(p_parts)
    y_stacks = cross_rows(before[chunks - 1 :])

    parts = [
        [p[0]] + [swap(p[d], "prow", d) for d in range(1, levels)] for p in parts
    ]
    sums = []
    for received in parts:
        if len(sums) == chunks - 1:
            received, y_stacks = lax.optimization_barrier((received, y_stacks))
        sums, received = lax.optimization_barrier((sums, received))
        total = sum((p.astype(f32) for p in received[1:]), received[0])
        sums = sums + [total.astype(bf16)]

    half = levels // 2
    sums = join(sums)
    pieces = [sums] + [swap(sums, "prow", d) for d in range(1, levels)]
    early = pieces[:half]
    early_across = [gather_x(p) for p in early]
    late, early_across, y_stacks = lax.optimization_barrier(
        (pieces[half:], early_across, y_stacks)
    )
    y_stacks = y_stacks + [swap(y, "pcol", 1) for y in y_stacks]
    own_rows = lay_rows(y_stacks, chunks, ids)
    late = jnp.concatenate(late, 0)
    late_across = gather_x(late)
    early = jnp.concatenate(early, 0)
    early_across = {e: jnp.concatenate([a[e] for a in early_across], 0) for e in late_across}
    take = functools.partial(take_off, pivot_inverse, levels=levels, ids=ids)
    one = lambda stacks: [[p] for p in stacks]
    if per_node == 2:
        pivot = take([(0, 0, one(gather_core({0: early}))), (1, 0, one(gather_core(early_across)))])
        pivot = take([(0, 1, one(gather_core({0: late})))], rest=pivot)
        late_across, pivot, own_rows = lax.optimization_barrier((late_across, pivot, own_rows))
        pivot = take([(1, 1, one(gather_core(late_across)))], rest=pivot)
    else:
        early = one(gather_core({0: early} | early_across))
        late = one(gather_core({0: late} | late_across))
        pivot = take(
            [
                (flip, half, part[flip * per_node : (flip + 1) * per_node])
                for flip in range(2)
                for half, part in enumerate((early, late))
            ]
        )
    return own_rows, pivot


def solution(mesh):
    in_specs = (
        P(None, ("pole", "prow"), "pcol"),
        P(("pole", "prow"), None, None),
        P("pole", "prow"),
        P("pole", None, None, None),
    )
    out_specs = (P(("pole", "prow", "pcol"), None, None), P("pole", None, None, None))
    return jax.shard_map(
        per_device, mesh=mesh, in_specs=in_specs, out_specs=out_specs, check_vma=False
    )
```
